512 devices in a mesh: req: 16 (over y, core), cand: 32 (over x, z).
Axes of the slice: x: 4, y: 8, z: 8, core: 2. Of those that a mesh axis runs over, the one named last changes fastest.
Arguments:
- cand_rows: bfloat16 [16, 16384, 512], P('req', 'cand'), may hold values from -6 to 6
- user_rows: bfloat16 [16, 64, 512], P('req', 'cand'), may hold values from -6 to 6
- row_owner: int32 [16, 16384, 1], P('req', 'cand'), may hold values from 0 to 31; in each aligned block of 512 rows (0 to 511, 512 to 1023, ..., all dimensions but the last counted through in order) at most 32 rows name the same one
- row_list: int32 [16, 16384], P('req', 'cand'), may hold values from 0 to 1
- cross_weight: bfloat16 [512, 512], replicated, may hold values from -0.25 to 0.25
- up_weight: bfloat16 [512, 1024], replicated, may hold values from -0.25 to 0.25
- down_weight: bfloat16 [1024, 512], replicated, may hold values from -0.1875 to 0.1875
- project_in: bfloat16 [512, 1536], P('req'), may hold values from -0.25 to 0.25
- project_out: bfloat16 [512, 512], replicated, may hold values from -0.25 to 0.25
Outputs:
- reranked: bfloat16 [16, 16384, 512], P('req', 'cand')
The draws below stay inside these ranges and needn't reach their ends.
Inputs may be any that keep to these rules, and one draw needn't show every extreme that they name: `row_owner`: among the rows of one device, at most 32 name the same owner, and some device of every draw has an owner named exactly 32 times.
All inputs are finite; a program needn't handle non-finite values.
Results may differ from the reference program's by a relative error of at most 0.0068.
Values may be sent and summed in bfloat16 or wider, within the bound.
No kernel may reach another device: no remote copies, remote signals or barrier semaphores. Data moves between devices by JAX's collectives and lax.ppermute only.
A program may use at most 64 MiB of HBM per device.

```python
import math
import jax
import jax.numpy as jnp
import numpy as np
from jax import lax

D = 512
H = 1024
HEADS = 8
LISTS_DEV = 2
ROWS_DEV = 512
CAPACITY = 32
NGROUPS = 16
ROWS_GRP = 16384
USERS_GRP = 64
N_CAND = 32


def place_ends(entries, own_key, least, largest):
    longest = entries.shape.index(max(entries.shape))
    spots = []
    for shift in (0, 1):
        where = [jax.random.randint(jax.random.fold_in(own_key, axis), (), 0, length) for axis, length in enumerate(entries.shape)]
        where[longest] = (where[longest] + shift) % entries.shape[longest]
        spots.append(tuple(where))
    return entries.at[spots[0]].set(least).at[spots[1]].set(largest)


def shard_levels(key, shape, shards, low, high):
    level, own = 1.0, jax.random.fold_in(key, 6)
    for dim, blocks in shards:
        steps = jnp.exp(jax.random.uniform(jax.random.fold_in(own, dim), (blocks,), jnp.float32, low / len(shards), high / len(shards)))
        level = level * jnp.repeat(steps, shape[dim] // blocks).reshape([-1 if axis == dim else 1 for axis in range(len(shape))])
    return level


def routed_block(own_key, own, number, rows, amount, top, bound, skew):
    order = jax.random.permutation(own_key, amount)
    crowded, common = portions_of(amount, rows * top, bound, skew, True), portions_of(amount, rows * top, bound, skew, False)
    places = jnp.arange(amount)

    def named(sizes, turn):
        used = int((sizes > 0).sum())
        fixed = max(1, used // 4)
        moved = fixed + (places - fixed + turn * (used - fixed)) % max(1, amount - fixed)
        return jnp.zeros((amount,), jnp.int32).at[order[jnp.where(places < fixed, places, moved)]].set(jnp.asarray(sizes, jnp.int32))

    sizes = jnp.where(number % 4 == 0, named(crowded, number // 4), named(common, number - number // 4 - 1))
    mixed = jax.random.permutation(jax.random.fold_in(own, 3), amount)
    giver, receiver = mixed[0:amount // 2 * 2:2], mixed[1:amount // 2 * 2:2]
    margin = jnp.minimum(sizes[giver] - 1, bound - sizes[receiver]) // 2
    margin = jnp.where((giver == order[0]) | (receiver == order[0]) | (sizes[receiver] == 0), 0, jnp.maximum(margin, 0))
    moved = jax.random.randint(jax.random.fold_in(own, 4), (amount // 2,), 0, 1 << 20) % (margin + 1)
    sizes = sizes.at[giver].add(-moved).at[receiver].add(moved)
    labels = jnp.searchsorted(jnp.cumsum(sizes), jnp.arange(rows * top), side="right").astype(jnp.int32)
    listing = labels.reshape(top, rows).T
    listing = listing[jax.random.permutation(jax.random.fold_in(own, 1), rows)]
    turn = jax.random.randint(jax.random.fold_in(own, 2), (rows, 1), 0, top)
    return jnp.take_along_axis(listing, (jnp.arange(top)[None, :] + turn) % top, axis=1)


def portions_of(number_of, total, limit, slope, full):
    portions = [(1 << 20) // math.isqrt(rank ** slope) + 1 for rank in range(1, number_of + 1)]
    largest = limit if full else min(limit, max(-(-total // number_of), total * portions[0] // sum(portions)))
    least = 1 if total - largest >= number_of - 1 else 0
    holding, spare = [largest] + [least] * (number_of - 1), total - largest - least * (number_of - 1)
    while spare > 0:
        free = [i for i in range(1, number_of) if holding[i] < largest] or [i for i in range(1, number_of) if holding[i] < limit]
        mass, left = sum([portions[i] for i in free]), spare
        for i in free:
            extra = min(limit - holding[i], max(1, left * portions[i] // mass), spare)
            holding[i] = holding[i] + extra
            spare = spare - extra
    return np.array(holding)


def gaussian(stream_key, shape, width, bound, cuts=(), kind=jnp.bfloat16):
    drawn = width * jax.random.normal(stream_key, shape, jnp.float32)
    if cuts:
        drawn = drawn * shard_levels(stream_key, shape, cuts, -0.22, 0.18)
    return jnp.clip(drawn, -bound, bound).astype(kind)


def setup_inputs(seed: int = 0) -> dict:
    seeds = jax.random.split(jax.random.key(seed), 10)
    cand_rows = gaussian(seeds[0], (NGROUPS, ROWS_GRP, D), 1.0, 6.0, ((0, 16), (1, 32)))
    user_rows = gaussian(seeds[1], (NGROUPS, USERS_GRP, D), 1.0, 6.0, ((0, 16), (1, 32)))
    row_owner_keys = jax.random.split(jax.random.fold_in(seeds[2], 1), NGROUPS * ROWS_GRP // ROWS_DEV)
    row_owner_turns = jax.random.permutation(jax.random.fold_in(seeds[2], 3), NGROUPS * ROWS_GRP // ROWS_DEV)
    row_owner = jax.vmap(lambda own, number: routed_block(jax.random.fold_in(seeds[2], 2), own, number, ROWS_DEV, N_CAND, 1, CAPACITY, 1))(row_owner_keys, row_owner_turns).reshape((NGROUPS, ROWS_GRP, 1))
    row_list = place_ends(jax.random.randint(seeds[3], (NGROUPS, ROWS_GRP), 0, LISTS_DEV), jax.random.fold_in(seeds[3], 1), 0, LISTS_DEV - 1).astype(jnp.int32)
    cross_weight = gaussian(seeds[4], (D, D), D ** -0.5, 0.25)
    up_weight = gaussian(seeds[5], (D, H), D ** -0.5, 0.25)
    down_weight = gaussian(seeds[6], (H, D), H ** -0.5, 0.1875)
    project_in = gaussian(seeds[7], (D, 3 * D), D ** -0.5, 0.25, ((0, 16),))
    project_out = gaussian(seeds[8], (D, D), D ** -0.5, 0.25)
    return {"cand_rows": cand_rows, "user_rows": user_rows, "row_owner": row_owner, "row_list": row_list, "cross_weight": cross_weight, "up_weight": up_weight, "down_weight": down_weight, "project_in": project_in, "project_out": project_out}


def layers(combined, cross_weight, up_weight, down_weight):
    wide = combined.astype(jnp.float32)
    crossed = (wide * jnp.dot(combined, cross_weight, preferred_element_type=jnp.float32) + wide).astype(jnp.bfloat16)
    activated = jax.nn.relu(jnp.dot(crossed, up_weight, preferred_element_type=jnp.float32)).astype(jnp.bfloat16)
    return (crossed.astype(jnp.float32) + jnp.dot(activated, down_weight, preferred_element_type=jnp.float32)).astype(jnp.bfloat16)

def project(mixed_rows, project_in):
    buffer_rows, model_width = mixed_rows.shape
    projected = jnp.dot(mixed_rows, project_in, preferred_element_type=jnp.float32)

    def normed(block):
        split = block.reshape(buffer_rows, HEADS, model_width // HEADS)
        split = split * lax.rsqrt(lax.optimization_barrier(jnp.mean(split * split, axis=-1, keepdims=True)) + 1e-06)
        return split.reshape(buffer_rows, model_width).astype(jnp.bfloat16)
    queries = normed(projected[:, :model_width])
    keys_all = normed(projected[:, model_width:2 * model_width])
    values_all = projected[:, 2 * model_width:].astype(jnp.bfloat16)
    return (queries, keys_all, values_all)

def attend(mixed_rows, queries, keys_all, values_all, list_tags, project_out):
    buffer_rows, model_width = mixed_rows.shape
    head_width = model_width // HEADS
    score_scale = head_width ** (-0.5)
    same_list = list_tags[:, None] == list_tags[None, :]

    def one_head(head_index):
        start = (head_index * head_width).astype(jnp.int32)
        query_part = lax.dynamic_slice_in_dim(queries, start, head_width, 1)
        key_part = lax.dynamic_slice_in_dim(keys_all, start, head_width, 1)
        value_part = lax.dynamic_slice_in_dim(values_all, start, head_width, 1)
        scores = jnp.dot(query_part, key_part.T, preferred_element_type=jnp.float32) * score_scale
        powered = jnp.where(same_list, jnp.exp(scores), jnp.float32(0.0))
        weights = (powered / lax.optimization_barrier(jnp.sum(powered, axis=1, keepdims=True))).astype(jnp.bfloat16)
        return jnp.dot(weights, value_part, preferred_element_type=jnp.float32).astype(jnp.bfloat16)
    per_head = lax.map(one_head, jnp.arange(HEADS, dtype=jnp.int32))
    attended = per_head.transpose(1, 0, 2).reshape(buffer_rows, model_width)
    return (mixed_rows.astype(jnp.float32) + jnp.dot(attended, project_out, preferred_element_type=jnp.float32)).astype(jnp.bfloat16)

def reference(cand_rows, user_rows, row_owner, row_list, cross_weight, up_weight, down_weight, project_in, project_out):
    total_slots = N_CAND * N_CAND * CAPACITY

    def per_group(group):
        rows_in, users_in, owners, lists = group
        owners = owners[:, 0]
        blocks = owners.reshape(N_CAND, ROWS_DEV)
        onehot = (blocks[:, :, None] == jnp.arange(N_CAND, dtype=jnp.int32)[None, None, :]).astype(jnp.int32)
        slot_rank = (lax.optimization_barrier(jnp.sum(jnp.cumsum(onehot, axis=1) * onehot, axis=-1)) - 1).reshape(-1)
        source = jnp.arange(ROWS_GRP, dtype=jnp.int32) // ROWS_DEV
        position = owners * (N_CAND * CAPACITY) + source * CAPACITY + slot_rank
        user_index = owners * LISTS_DEV + lists
        combined = (rows_in.astype(jnp.float32) + users_in[user_index].astype(jnp.float32)).astype(jnp.bfloat16)
        mixed_rows = layers(combined, cross_weight, up_weight, down_weight)
        buffer = jnp.zeros((total_slots, D), jnp.bfloat16).at[position].set(mixed_rows)
        list_tags = jnp.zeros((total_slots,), jnp.int32).at[position].set(lists + 1)

        def per_owner(item):
            owner_rows, owner_tags = item
            queries, keys_all, values_all = project(owner_rows, project_in)
            return attend(owner_rows, queries, keys_all, values_all, owner_tags, project_out)
        result = lax.map(per_owner, (buffer.reshape(N_CAND, N_CAND * CAPACITY, D), list_tags.reshape(N_CAND, N_CAND * CAPACITY)))
        return result.reshape(total_slots, D)[position]
    return lax.map(per_group, (cand_rows, user_rows, row_owner, row_list))
```

```python
import jax
import jax.numpy as jnp
from jax import lax
from jax.experimental import pallas as pl
from jax.experimental.pallas import tpu as pltpu
from jax.sharding import PartitionSpec as P

HEADS = 8
PEERS = 32
CAP = 32
SLOTS = PEERS * CAP
D = 512
LANES = 128
COLS = D // LANES
PAY = COLS * CAP + 8
BLOCK = 256
APART = 1024.0
BF = jnp.bfloat16
F32 = jnp.float32
VMEM = pl.BlockSpec(memory_space=pltpu.VMEM)
NT = (((1,), (1,)), ((), ()))


def iota(shape, dim):
    return lax.broadcasted_iota(jnp.int32, shape, dim)


def ones_where(cond):
    return jnp.where(cond, 1.0, 0.0).astype(BF)


def dot(a, b):
    return jnp.dot(a, b, preferred_element_type=F32)


def pack_kernel(rows_ref, owner_ref, list_ref, pay_ref, pos_ref):
    rows = rows_ref.shape[0]
    owner = owner_ref[...]
    mine = iota((PEERS, rows), 0) == owner
    upto = ones_where(iota((rows, rows), 0) <= iota((rows, rows), 1))
    count = dot(ones_where(mine), upto)
    rank = jnp.sum(jnp.where(mine, count, 0.0), axis=0, keepdims=True).astype(jnp.int32) - 1
    pos = owner * CAP + rank
    pos_ref[...] = pos
    half = SLOTS // 2
    for part in range(2):
        place = ones_where(iota((half, rows), 0) + part * half == pos)
        sent = dot(place, rows_ref[...]).astype(BF)
        peers = pl.ds(part * (PEERS // 2), PEERS // 2)
        for c in range(COLS):
            pay_ref[peers, c * CAP : (c + 1) * CAP, :] = sent[:, c * LANES : (c + 1) * LANES].reshape(
                PEERS // 2, CAP, LANES
            )
    tags = jnp.where(mine, (list_ref[...] + 1).astype(F32), 0.0).astype(BF)
    at_rank = ones_where(iota((LANES, rows), 0) == rank)
    tag_rows = lax.dot_general(tags, at_rank, NT, preferred_element_type=F32)
    pay_ref[:, COLS * CAP :, :] = jnp.broadcast_to(
        tag_rows[:, None, :], (PEERS, PAY - COLS * CAP, LANES)
    ).astype(BF)


def pack(rows, owner, lists):
    return pl.pallas_call(
        pack_kernel,
        out_shape=(
            jax.ShapeDtypeStruct((PEERS, PAY, LANES), BF),
            jax.ShapeDtypeStruct(owner.shape, jnp.int32),
        ),
        in_specs=[VMEM] * 3,
        out_specs=(VMEM, VMEM),
        name="pack_rows",
        cost_estimate=pl.CostEstimate(flops=2**29, bytes_accessed=2**21, transcendentals=0),
    )(rows, owner, lists)


def pick_kernel(pos_ref, pick_ref):
    rows = pick_ref.shape[0]
    pos = pos_ref[...].astype(F32)
    column = jnp.sum(
        jnp.where(iota((rows, rows), 0) == iota((rows, rows), 1), pos, 0.0), axis=1, keepdims=True
    ).astype(jnp.int32)
    pick_ref[...] = ones_where(iota(pick_ref.shape, 1) == column)


def pick_matrix(pos):
    return pl.pallas_call(
        pick_kernel,
        out_shape=jax.ShapeDtypeStruct((pos.shape[1], SLOTS), BF),
        in_specs=[VMEM],
        out_specs=VMEM,
        name="pick_matrix",
        cost_estimate=pl.CostEstimate(flops=2**28, bytes_accessed=2**20, transcendentals=0),
    )(pos)


def unpick_kernel(pick_ref, back_ref, out_ref):
    out_ref[...] = dot(pick_ref[...], back_ref[...]).astype(BF)


def unpick(pick, back):
    return pl.pallas_call(
        unpick_kernel,
        out_shape=jax.ShapeDtypeStruct((pick.shape[0], D), BF),
        in_specs=[VMEM] * 2,
        out_specs=VMEM,
        name="unpick_rows",
        cost_estimate=pl.CostEstimate(flops=2**29, bytes_accessed=2**21, transcendentals=0),
    )(pick, back)


def main_kernel(
    y_ref,
    pay_ref,
    user_ref,
    cross_ref,
    up_ref,
    down_ref,
    near_ref,
    far_ref,
    out_w_ref,
    out_ref,
    mixed_ref,
    in_ref,
    even_q,
    odd_q,
    even_k,
    odd_k,
    values_ref,
):
    share = near_ref.shape[0] // 8
    y, core = y_ref[0], y_ref[1]
    for i, step in enumerate((1, 0, -1, -2, -3, -4, 3, 2)):
        chip = lax.rem(y + step + 8, 8) * 2
        for ref, which in ((near_ref, core), (far_ref, 1 - core)):
            spot = pl.multiple_of((chip + which) * share, share)
            in_ref[pl.ds(spot, share), :] = ref[i * share : (i + 1) * share, :]

    low = iota((BLOCK, LANES), 1) < LANES // 2
    lane = iota((BLOCK, LANES), 1)
    fit = lane == lax.rem(iota((BLOCK, LANES), 0), CAP)
    spread = ones_where(iota((LANES, LANES), 0) >= 0)
    head = D // HEADS
    mean = jnp.where(
        iota((BLOCK, BLOCK), 0) // head == iota((BLOCK, BLOCK), 1) // head, 1.0 / head, 0.0
    ).astype(BF)
    ones_low = ones_where(low)
    ones_high = ones_where(jnp.logical_not(low))

    def normed(block, scale):
        square = (block * block).astype(BF)
        parts = []
        for j in range(D // BLOCK):
            cut = slice(j * BLOCK, (j + 1) * BLOCK)
            parts.append(block[:, cut] * (lax.rsqrt(dot(square[:, cut], mean) + 1e-06) * scale))
        return jnp.concatenate(parts, axis=1)

    def prepare(b, carry):
        peers = pl.ds(b * (BLOCK // CAP), BLOCK // CAP)
        rows = pl.ds(pl.multiple_of(b * BLOCK, BLOCK), BLOCK)
        tag8 = pay_ref[peers, COLS * CAP :, :].astype(F32)
        tag32 = jnp.concatenate([tag8] * (CAP // 8), axis=1).reshape(BLOCK, LANES)
        tag = dot(jnp.where(fit, tag32, 0.0).astype(BF), spread)
        first, second = tag == 1.0, tag == 2.0
        combined = []
        for c in range(COLS):
            cut = slice(c * LANES, (c + 1) * LANES)
            x = pay_ref[peers, c * CAP : (c + 1) * CAP, :].reshape(BLOCK, LANES).astype(F32)
            user = jnp.where(second, user_ref[1:2, cut].astype(F32), user_ref[0:1, cut].astype(F32))
            combined.append((x + user).astype(BF))
        combined = jnp.concatenate(combined, axis=1)
        wide = combined.astype(F32)
        crossed = (wide * dot(combined, cross_ref[...]) + wide).astype(BF)
        active = jnp.maximum(dot(crossed, up_ref[...]), 0.0).astype(BF)
        mixed = (crossed.astype(F32) + dot(active, down_ref[...])).astype(BF)
        mixed_ref[rows, :] = mixed
        queries = normed(dot(mixed, in_ref[:, :D]), head**-0.5)
        keys = normed(dot(mixed, in_ref[:, D : 2 * D]), 1.0)
        values = dot(mixed, in_ref[:, 2 * D :]).astype(BF)

        odd_lane = lax.rem(lane, LANES // 2)
        query_mark = jnp.where(
            jnp.logical_or(
                jnp.logical_and(odd_lane == 0, first), jnp.logical_and(odd_lane == 1, second)
            ),
            -APART,
            0.0,
        )
        key_mark = jnp.where(
            jnp.logical_or(
                jnp.logical_and(odd_lane == 0, jnp.logical_not(first)),
                jnp.logical_and(odd_lane == 1, jnp.logical_not(second)),
            ),
            1.0,
            0.0,
        )
        for p in range(HEADS // 2):
            cut = slice(p * LANES, (p + 1) * LANES)
            even_q[rows, cut] = jnp.where(low, queries[:, cut], query_mark).astype(BF)
            odd_q[rows, cut] = jnp.where(low, query_mark, queries[:, cut]).astype(BF)
            even_k[rows, cut] = jnp.where(low, keys[:, cut], key_mark).astype(BF)
            odd_k[rows, cut] = jnp.where(low, key_mark, keys[:, cut]).astype(BF)
            value = values[:, cut].astype(F32)
            values_ref[p, rows, :LANES] = jnp.where(low, value, 0.0).astype(BF)
            values_ref[p, rows, LANES:] = ones_low
            later = pl.ds(pl.multiple_of(SLOTS + b * BLOCK, BLOCK), BLOCK)
            values_ref[p, later, :LANES] = jnp.where(low, 0.0, value).astype(BF)
            values_ref[p, later, LANES:] = ones_high
        return carry

    lax.fori_loop(0, SLOTS // BLOCK, prepare, 0)

    def attend(b, carry):
        rows = pl.ds(pl.multiple_of(b * BLOCK, BLOCK), BLOCK)
        attended = []
        for p in range(HEADS // 2):
            cut = slice(p * LANES, (p + 1) * LANES)
            powered = []
            for q, k in ((even_q, even_k), (odd_q, odd_k)):
                score = lax.dot_general(q[rows, cut], k[:, cut], NT, preferred_element_type=F32)
                powered.append(jnp.exp(score).astype(BF))
            summed = dot(powered[0], values_ref[p, :SLOTS, :]) + dot(
                powered[1], values_ref[p, SLOTS:, :]
            )
            attended.append((summed[:, :LANES] / summed[:, LANES:]).astype(BF))
        attended = jnp.concatenate(attended, axis=1)
        out_ref[rows, :] = (
            mixed_ref[rows, :].astype(F32) + dot(attended, out_w_ref[...])
        ).astype(BF)
        return carry

    lax.fori_loop(0, SLOTS // BLOCK, attend, 0)


def rerank(place, pay, users, cross, up, down, near, far, out_w):
    wide = pltpu.VMEM((SLOTS, D), BF)
    return pl.pallas_call(
        main_kernel,
        out_shape=jax.ShapeDtypeStruct((SLOTS, D), BF),
        in_specs=[pl.BlockSpec(memory_space=pltpu.SMEM)] + [VMEM] * 8,
        out_specs=VMEM,
        scratch_shapes=[
            wide,
            pltpu.VMEM((D, 3 * D), BF),
            wide,
            wide,
            wide,
            wide,
            pltpu.VMEM((HEADS // 2, 2 * SLOTS, 2 * LANES), BF),
        ],
        compiler_params=pltpu.CompilerParams(vmem_limit_bytes=48 * 2**20),
        name="rerank_lists",
        cost_estimate=pl.CostEstimate(flops=2**34, bytes_accessed=2**23, transcendentals=2**23),
    )(place, pay, users, cross, up, down, near, far, out_w)


def exchange(values):
    return lax.all_to_all(values, "cand", split_axis=0, concat_axis=0, tiled=True)


def along_y(steps):
    return [(i, (i + 2 * steps) % 16) for i in range(16)]


def gather_projection(part):
    share = part.shape[0]
    back = lax.ppermute(part, "req", along_y(1))
    ahead = lax.ppermute(part, "req", along_y(7))
    three = jnp.concatenate([ahead, part, back], axis=0)
    behind = lax.ppermute(three, "req", along_y(3))
    front = lax.ppermute(three[share:], "req", along_y(5))
    near = jnp.concatenate([three, behind, front], axis=0)
    far = lax.ppermute(near, "req", [(i, i ^ 1) for i in range(16)])
    return near, far


def local(
    cand_rows,
    user_rows,
    row_owner,
    row_list,
    cross_weight,
    up_weight,
    down_weight,
    project_in,
    project_out,
):
    pay, pos = pack(cand_rows[0], row_owner.reshape(1, -1), row_list)
    arrived = exchange(pay)
    near, far = gather_projection(project_in)
    pick = pick_matrix(pos)
    req = lax.axis_index("req")
    place = jnp.stack([req // 2, req % 2]).astype(jnp.int32)
    result = rerank(
        place, arrived, user_rows[0], cross_weight, up_weight, down_weight, near, far, project_out
    )
    back = exchange(result.reshape(PEERS, CAP, D))
    return unpick(pick, back.reshape(SLOTS, D))[None]


def solution(mesh):
    in_specs = (
        P("req", "cand", None),
        P("req", "cand", None),
        P("req", "cand", None),
        P("req", "cand"),
        P(),
        P(),
        P(),
        P("req", None),
        P(),
    )
    out_specs = P("req", "cand", None)
    return jax.shard_map(local, mesh=mesh, in_specs=in_specs, out_specs=out_specs, check_vma=False)
```

```python
import jax
import jax.numpy as jnp
from jax import lax
from jax.experimental import pallas as pl
from jax.experimental.pallas import tpu as pltpu
from jax.sharding import PartitionSpec as P

HEADS = 8
PEERS = 32
CAP = 32
SLOTS = PEERS * CAP
D = 512
LANES = 128
COLS = D // LANES
PAY = COLS * CAP + 8
QBLOCK = 512
APART = 1024.0
BF = jnp.bfloat16
F32 = jnp.float32
VMEM = pl.BlockSpec(memory_space=pltpu.VMEM)
STEPS = (0, 4, 1, 5, 7, 3, 2, 6)
NT = (((1,), (1,)), ((), ()))


def iota(shape, dim):
    return lax.broadcasted_iota(jnp.int32, shape, dim)


def ones_where(cond):
    return jnp.where(cond, 1.0, 0.0).astype(BF)


def dot(a, b):
    return jnp.dot(a, b, preferred_element_type=F32)


def pack_kernel(rows_ref, owner_ref, list_ref, pay_ref, pos_ref):
    rows = rows_ref.shape[0]
    owner = owner_ref[...]
    mine = iota((PEERS, rows), 0) == owner
    upto = ones_where(iota((rows, rows), 0) <= iota((rows, rows), 1))
    count = dot(ones_where(mine), upto)
    rank = jnp.sum(jnp.where(mine, count, 0.0), axis=0, keepdims=True).astype(jnp.int32) - 1
    pos = owner * CAP + rank
    pos_ref[...] = pos
    half = SLOTS // 2
    for part in range(2):
        place = ones_where(iota((half, rows), 0) + part * half == pos)
        sent = dot(place, rows_ref[...]).astype(BF)
        peers = pl.ds(part * (PEERS // 2), PEERS // 2)
        for c in range(COLS):
            pay_ref[peers, c * CAP : (c + 1) * CAP, :] = sent[:, c * LANES : (c + 1) * LANES].reshape(
                PEERS // 2, CAP, LANES
            )
    tags = jnp.where(mine, (list_ref[...] + 1).astype(F32), 0.0).astype(BF)
    at_rank = ones_where(iota((LANES, rows), 0) == rank)
    tag_rows = lax.dot_general(tags, at_rank, NT, preferred_element_type=F32)
    pay_ref[:, COLS * CAP :, :] = jnp.broadcast_to(
        tag_rows[:, None, :], (PEERS, PAY - COLS * CAP, LANES)
    ).astype(BF)


def pack(rows, owner, lists):
    return pl.pallas_call(
        pack_kernel,
        out_shape=(
            jax.ShapeDtypeStruct((PEERS, PAY, LANES), BF),
            jax.ShapeDtypeStruct(owner.shape, jnp.int32),
        ),
        in_specs=[VMEM] * 3,
        out_specs=(VMEM, VMEM),
        name="pack_rows",
        cost_estimate=pl.CostEstimate(flops=2**29, bytes_accessed=2**21, transcendentals=0),
    )(rows, owner, lists)


def pick_kernel(pos_ref, pick_ref):
    rows = pick_ref.shape[0]
    pos = pos_ref[...].astype(F32)
    column = jnp.sum(
        jnp.where(iota((rows, rows), 0) == iota((rows, rows), 1), pos, 0.0), axis=1, keepdims=True
    ).astype(jnp.int32)
    pick_ref[...] = ones_where(iota(pick_ref.shape, 1) == column)


def pick_matrix(pos):
    return pl.pallas_call(
        pick_kernel,
        out_shape=jax.ShapeDtypeStruct((pos.shape[1], SLOTS), BF),
        in_specs=[VMEM],
        out_specs=VMEM,
        name="pick_matrix",
        cost_estimate=pl.CostEstimate(flops=2**36, bytes_accessed=2**28, transcendentals=0),
    )(pos)


def main_kernel(
    y_ref,
    pay_ref,
    user_ref,
    cross_ref,
    up_ref,
    down_ref,
    *refs,
):
    part_refs, (out_w_ref, out_ref) = refs[:8], refs[8:10]
    mixed_ref, in_ref, in_t, even_k, odd_k, queries_ref, values_ref, attended_ref = refs[10:]
    share = part_refs[0].shape[0] // 2
    y, core = y_ref[0], y_ref[1]
    for i, step in enumerate(STEPS):
        chip = lax.rem(y + step, 8) * 2
        for ref, which in ((part_refs[i // 2], core), (part_refs[4 + i // 2], 1 - core)):
            spot = pl.multiple_of((chip + which) * share, share)
            in_ref[pl.ds(spot, share), :] = ref[i % 2 * share : (i % 2 + 1) * share, :]

    in_t[...] = jnp.concatenate([in_ref[:, :D].T, in_ref[:, 2 * D :].T], axis=0)

    head = D // HEADS
    lane = iota((SLOTS, LANES), 1)
    low = lane < head
    fit = lane == lax.rem(iota((SLOTS, LANES), 0), CAP)
    spread = ones_where(iota((LANES, LANES), 0) >= 0)
    mean = jnp.where(
        iota((256, 256), 0) // head == iota((256, 256), 1) // head, 1.0 / head, 0.0
    ).astype(BF)

    tag8 = pay_ref[:, COLS * CAP :, :].astype(F32)
    tag32 = jnp.concatenate([tag8] * (CAP // 8), axis=1).reshape(SLOTS, LANES)
    tag_bf = jnp.where(fit, tag32, 0.0).astype(BF)
    tag = dot(tag_bf, spread)
    tag_t = lax.dot_general(spread[:head], tag_bf, NT, preferred_element_type=F32)
    first, second = tag == 1.0, tag == 2.0
    combined = []
    for c in range(COLS):
        cut = slice(c * LANES, (c + 1) * LANES)
        x = pay_ref[:, c * CAP : (c + 1) * CAP, :].reshape(SLOTS, LANES).astype(F32)
        user = jnp.where(second, user_ref[1:2, cut].astype(F32), user_ref[0:1, cut].astype(F32))
        combined.append((x + user).astype(BF))
    combined = jnp.concatenate(combined, axis=1)
    wide = combined.astype(F32)
    crossed = (wide * dot(combined, cross_ref[...]) + wide).astype(BF)
    active = jnp.maximum(dot(crossed, up_ref[...]), 0.0).astype(BF)
    mixed = (crossed.astype(F32) + dot(active, down_ref[...])).astype(BF)
    mixed_ref[...] = mixed

    keys = dot(mixed, in_ref[:, D : 2 * D])
    square = (keys * keys).astype(BF)
    spot = lax.rem(lane, head)
    key_mark = jnp.where(
        jnp.logical_or(
            jnp.logical_and(spot == 0, jnp.logical_not(first)),
            jnp.logical_and(spot == 1, jnp.logical_not(second)),
        ),
        1.0,
        0.0,
    )
    for j in range(D // 256):
        cut = slice(j * 256, (j + 1) * 256)
        normed = keys[:, cut] * lax.rsqrt(dot(square[:, cut], mean) + 1e-06)
        for i in range(2):
            key = normed[:, i * LANES : (i + 1) * LANES]
            even_k[2 * j + i, :, :] = jnp.where(low, key, key_mark).astype(BF)
            odd_k[2 * j + i, :, :] = jnp.where(low, key_mark, key).astype(BF)

    turned = lax.dot_general(in_t[...], mixed, NT, preferred_element_type=F32)
    row = iota((head, SLOTS), 0)
    query_mark = jnp.where(
        jnp.logical_or(
            jnp.logical_and(row == 0, tag_t == 1.0), jnp.logical_and(row == 1, tag_t == 2.0)
        ),
        -APART,
        0.0,
    ).astype(BF)
    for h in range(HEADS):
        query = turned[h * head : (h + 1) * head, :]
        level = jnp.mean(query * query, axis=0, keepdims=True)
        query = (query * (lax.rsqrt(level + 1e-06) * head**-0.5)).astype(BF)
        at = h % 2 * head
        queries_ref[h, at : at + head, :] = query
        queries_ref[h, head - at : 2 * head - at, :] = query_mark
        values_ref[h, :head, :] = turned[D + h * head : D + (h + 1) * head, :].astype(BF)
        values_ref[h, head:, :] = ones_where(iota((16, SLOTS), 0) >= 0)

    for p in range(HEADS // 2):
        pair = []
        for i, k in enumerate((even_k, odd_k)):
            h = 2 * p + i
            halves = []
            for j in range(SLOTS // QBLOCK):
                cut = slice(j * QBLOCK, (j + 1) * QBLOCK)
                powered = jnp.exp(dot(k[p], queries_ref[h, :, cut])).astype(BF)
                summed = dot(values_ref[h], powered)
                halves.append((summed[:head] / summed[head : head + 1]).astype(BF))
            pair.append(jnp.concatenate(halves, axis=1))
        attended_ref[p] = jnp.concatenate(pair, axis=0).T

    attended = jnp.concatenate([attended_ref[p] for p in range(HEADS // 2)], axis=1)
    out_ref[...] = (mixed_ref[...].astype(F32) + dot(attended, out_w_ref[...])).astype(BF)


def rerank(place, pay, users, cross, up, down, parts, out_w):
    wide = pltpu.VMEM((SLOTS, D), BF)
    pairs = pltpu.VMEM((HEADS // 2, SLOTS, LANES), BF)
    return pl.pallas_call(
        main_kernel,
        out_shape=jax.ShapeDtypeStruct((SLOTS, D), BF),
        in_specs=[pl.BlockSpec(memory_space=pltpu.SMEM)] + [VMEM] * (6 + len(parts)),
        out_specs=VMEM,
        scratch_shapes=[
            wide,
            pltpu.VMEM((D, 3 * D), BF),
            pltpu.VMEM((2 * D, D), BF),
            pairs,
            pairs,
            pltpu.VMEM((HEADS, LANES, SLOTS), BF),
            pltpu.VMEM((HEADS, D // HEADS + 16, SLOTS), BF),
            pairs,
        ],
        compiler_params=pltpu.CompilerParams(vmem_limit_bytes=48 * 2**20),
        name="rerank_lists",
        cost_estimate=pl.CostEstimate(flops=2**34, bytes_accessed=2**23, transcendentals=2**23),
    )(place, pay, users, cross, up, down, *parts, out_w)


def exchange(values):
    return lax.all_to_all(values, "cand", split_axis=0, concat_axis=0, tiled=True)


def along_y(steps):
    return [(i, (i + 2 * steps) % 16) for i in range(16)]


CORE = [(i, i ^ 1) for i in range(16)]


def gather_projection(part, opposite):
    pair = jnp.concatenate([part, opposite], axis=0)
    two = lax.ppermute(pair, "req", along_y(6))
    one = lax.ppermute(pair, "req", along_y(7))
    seven = lax.ppermute(pair, "req", along_y(1))
    near = (pair, one, seven, two)
    return near + tuple(lax.ppermute(piece, "req", CORE) for piece in near)


def local(
    cand_rows,
    user_rows,
    row_owner,
    row_list,
    cross_weight,
    up_weight,
    down_weight,
    project_in,
    project_out,
):
    opposite = lax.ppermute(project_in, "req", along_y(4))
    pay, pos = pack(cand_rows[0], row_owner.reshape(1, -1), row_list)
    arrived = exchange(pay)
    pick, opposite = lax.optimization_barrier((pick_matrix(pos), opposite))
    parts = gather_projection(project_in, opposite)
    req = lax.axis_index("req")
    place = jnp.stack([req // 2, req % 2]).astype(jnp.int32)
    result = rerank(
        place, arrived, user_rows[0], cross_weight, up_weight, down_weight, parts, project_out
    )
    back = exchange(result.reshape(PEERS, CAP, D))
    return dot(pick, back.reshape(SLOTS, D)).astype(BF)[None]


def solution(mesh):
    in_specs = (
        P("req", "cand", None),
        P("req", "cand", None),
        P("req", "cand", None),
        P("req", "cand"),
        P(),
        P(),
        P(),
        P("req", None),
        P(),
    )
    out_specs = P("req", "cand", None)
    return jax.shard_map(local, mesh=mesh, in_specs=in_specs, out_specs=out_specs, check_vma=False)
```

```python
import jax
import jax.numpy as jnp
from jax import lax
from jax.experimental import pallas as pl
from jax.experimental.pallas import tpu as pltpu
from jax.sharding import PartitionSpec as P

HEADS = 8
PEERS = 32
CAP = 32
SLOTS = PEERS * CAP
D = 512
LANES = 128
COLS = D // LANES
PAY = COLS * CAP + 8
QBLOCK = 512
APART = 1024.0
BF = jnp.bfloat16
F32 = jnp.float32
VMEM = pl.BlockSpec(memory_space=pltpu.VMEM)
ANY = pl.BlockSpec(memory_space=pl.ANY)
PARTS = 4
STEPS = (0, 4, 1, 5, 7, 3, 2, 6)
NT = (((1,), (1,)), ((), ()))


def iota(shape, dim):
    return lax.broadcasted_iota(jnp.int32, shape, dim)


def ones_where(cond):
    return jnp.where(cond, 1.0, 0.0).astype(BF)


def dot(a, b):
    return jnp.dot(a, b, preferred_element_type=F32)


def pack_kernel(rows_hbm, owner_hbm, list_hbm, pay_hbm, pos_hbm, rows_ref, owner_ref, list_ref, pay_ref, pos_ref, sems, sent_sems):
    fetch = [
        pltpu.make_async_copy(owner_hbm, owner_ref, sems.at[0]),
        pltpu.make_async_copy(list_hbm, list_ref, sems.at[1]),
        pltpu.make_async_copy(rows_hbm, rows_ref, sems.at[2]),
    ]
    for copy in fetch:
        copy.start()
    rows = rows_ref.shape[0]
    upto = ones_where(iota((rows, rows), 0) <= iota((rows, rows), 1))
    fetch[0].wait()
    owner = owner_ref[...]
    mine = iota((PEERS, rows), 0) == owner
    count = dot(ones_where(mine), upto)
    rank = jnp.sum(jnp.where(mine, count, 0.0), axis=0, keepdims=True).astype(jnp.int32) - 1
    pos = owner * CAP + rank
    pos_ref[...] = pos
    leave = [pltpu.make_async_copy(pos_ref, pos_hbm, sems.at[3])]
    leave[0].start()
    fetch[1].wait()
    tags = jnp.where(mine, (list_ref[...] + 1).astype(F32), 0.0).astype(BF)
    at_rank = ones_where(iota((LANES, rows), 0) == rank)
    tag_rows = lax.dot_general(tags, at_rank, NT, preferred_element_type=F32)
    pay_ref[:, COLS * CAP :, :] = jnp.broadcast_to(
        tag_rows[:, None, :], (PEERS, PAY - COLS * CAP, LANES)
    ).astype(BF)
    fetch[2].wait()
    for part in range(PARTS):
        width = SLOTS // PARTS
        place = ones_where(iota((width, rows), 0) + part * width == pos)
        sent = dot(place, rows_ref[...]).astype(BF)
        peers = pl.ds(part * (PEERS // PARTS), PEERS // PARTS)
        for c in range(COLS):
            pay_ref[peers, c * CAP : (c + 1) * CAP, :] = sent[:, c * LANES : (c + 1) * LANES].reshape(
                PEERS // PARTS, CAP, LANES
            )
        copy = pltpu.make_async_copy(pay_ref.at[peers], pay_hbm.at[peers], sent_sems.at[part])
        copy.start()
        leave.append(copy)
    for copy in leave:
        copy.wait()


def pack(rows, owner, lists):
    return pl.pallas_call(
        pack_kernel,
        out_shape=(
            jax.ShapeDtypeStruct((PEERS, PAY, LANES), BF),
            jax.ShapeDtypeStruct(owner.shape, jnp.int32),
        ),
        in_specs=[ANY] * 3,
        out_specs=(ANY, ANY),
        scratch_shapes=[
            pltpu.VMEM(rows.shape, BF),
            pltpu.VMEM(owner.shape, jnp.int32),
            pltpu.VMEM(lists.shape, jnp.int32),
            pltpu.VMEM((PEERS, PAY, LANES), BF),
            pltpu.VMEM(owner.shape, jnp.int32),
            pltpu.SemaphoreType.DMA((4,)),
            pltpu.SemaphoreType.DMA((PARTS,)),
        ],
        name="pack_rows",
        cost_estimate=pl.CostEstimate(flops=2**29, bytes_accessed=2**21, transcendentals=0),
    )(rows, owner, lists)


def pick_kernel(pos_ref, pick_ref):
    rows = pick_ref.shape[0]
    pos = pos_ref[...].astype(F32)
    column = jnp.sum(
        jnp.where(iota((rows, rows), 0) == iota((rows, rows), 1), pos, 0.0), axis=1, keepdims=True
    ).astype(jnp.int32)
    pick_ref[...] = ones_where(iota(pick_ref.shape, 1) == column)


def pick_matrix(pos):
    return pl.pallas_call(
        pick_kernel,
        out_shape=jax.ShapeDtypeStruct((pos.shape[1], SLOTS), BF),
        in_specs=[VMEM],
        out_specs=VMEM,
        name="pick_matrix",
        cost_estimate=pl.CostEstimate(flops=2**36, bytes_accessed=2**28, transcendentals=0),
    )(pos)


def main_kernel(
    y_ref,
    pay_ref,
    user_ref,
    cross_ref,
    up_ref,
    down_ref,
    *refs,
):
    part_refs, (out_w_ref, out_ref) = refs[:8], refs[8:10]
    mixed_ref, in_ref, in_t, even_k, odd_k, queries_ref, values_ref, attended_ref = refs[10:]
    share = part_refs[0].shape[0] // 2
    y, core = y_ref[0], y_ref[1]
    for i, step in enumerate(STEPS):
        chip = lax.rem(y + step, 8) * 2
        for ref, which in ((part_refs[i // 2], core), (part_refs[4 + i // 2], 1 - core)):
            spot = pl.multiple_of((chip + which) * share, share)
            in_ref[pl.ds(spot, share), :] = ref[i % 2 * share : (i % 2 + 1) * share, :]

    in_t[...] = jnp.concatenate([in_ref[:, :D].T, in_ref[:, 2 * D :].T], axis=0)

    head = D // HEADS
    lane = iota((SLOTS, LANES), 1)
    low = lane < head
    fit = lane == lax.rem(iota((SLOTS, LANES), 0), CAP)
    spread = ones_where(iota((LANES, LANES), 0) >= 0)
    mean = jnp.where(
        iota((256, 256), 0) // head == iota((256, 256), 1) // head, 1.0 / head, 0.0
    ).astype(BF)

    tag8 = pay_ref[:, COLS * CAP :, :].astype(F32)
    tag32 = jnp.concatenate([tag8] * (CAP // 8), axis=1).reshape(SLOTS, LANES)
    tag_bf = jnp.where(fit, tag32, 0.0).astype(BF)
    tag = dot(tag_bf, spread)
    tag_t = lax.dot_general(spread[:head], tag_bf, NT, preferred_element_type=F32)
    first, second = tag == 1.0, tag == 2.0
    combined = []
    for c in range(COLS):
        cut = slice(c * LANES, (c + 1) * LANES)
        x = pay_ref[:, c * CAP : (c + 1) * CAP, :].reshape(SLOTS, LANES).astype(F32)
        user = jnp.where(second, user_ref[1:2, cut].astype(F32), user_ref[0:1, cut].astype(F32))
        combined.append((x + user).astype(BF))
    combined = jnp.concatenate(combined, axis=1)
    wide = combined.astype(F32)
    crossed = (wide * dot(combined, cross_ref[...]) + wide).astype(BF)
    active = jnp.maximum(dot(crossed, up_ref[...]), 0.0).astype(BF)
    mixed = (crossed.astype(F32) + dot(active, down_ref[...])).astype(BF)
    mixed_ref[...] = mixed

    keys = dot(mixed, in_ref[:, D : 2 * D])
    square = (keys * keys).astype(BF)
    spot = lax.rem(lane, head)
    key_mark = jnp.where(
        jnp.logical_or(
            jnp.logical_and(spot == 0, jnp.logical_not(first)),
            jnp.logical_and(spot == 1, jnp.logical_not(second)),
        ),
        1.0,
        0.0,
    )
    for j in range(D // 256):
        cut = slice(j * 256, (j + 1) * 256)
        normed = keys[:, cut] * lax.rsqrt(dot(square[:, cut], mean) + 1e-06)
        for i in range(2):
            key = normed[:, i * LANES : (i + 1) * LANES]
            even_k[2 * j + i, :, :] = jnp.where(low, key, key_mark).astype(BF)
            odd_k[2 * j + i, :, :] = jnp.where(low, key_mark, key).astype(BF)

    turned = lax.dot_general(in_t[...], mixed, NT, preferred_element_type=F32)
    row = iota((head, SLOTS), 0)
    query_mark = jnp.where(
        jnp.logical_or(
            jnp.logical_and(row == 0, tag_t == 1.0), jnp.logical_and(row == 1, tag_t == 2.0)
        ),
        -APART,
        0.0,
    ).astype(BF)
    for h in range(HEADS):
        query = turned[h * head : (h + 1) * head, :]
        level = jnp.mean(query * query, axis=0, keepdims=True)
        query = (query * (lax.rsqrt(level + 1e-06) * head**-0.5)).astype(BF)
        at = h % 2 * head
        queries_ref[h, at : at + head, :] = query
        queries_ref[h, head - at : 2 * head - at, :] = query_mark
        values_ref[h, :head, :] = turned[D + h * head : D + (h + 1) * head, :].astype(BF)
        values_ref[h, head:, :] = ones_where(iota((16, SLOTS), 0) >= 0)

    for p in range(HEADS // 2):
        pair = []
        for i, k in enumerate((even_k, odd_k)):
            h = 2 * p + i
            halves = []
            for j in range(SLOTS // QBLOCK):
                cut = slice(j * QBLOCK, (j + 1) * QBLOCK)
                powered = jnp.exp(dot(k[p], queries_ref[h, :, cut])).astype(BF)
                summed = dot(values_ref[h], powered)
                halves.append((summed[:head] / summed[head : head + 1]).astype(BF))
            pair.append(jnp.concatenate(halves, axis=1))
        attended_ref[p] = jnp.concatenate(pair, axis=0).T

    attended = jnp.concatenate([attended_ref[p] for p in range(HEADS // 2)], axis=1)
    out_ref[...] = (mixed_ref[...].astype(F32) + dot(attended, out_w_ref[...])).astype(BF)


def rerank(place, pay, users, cross, up, down, parts, out_w):
    wide = pltpu.VMEM((SLOTS, D), BF)
    pairs = pltpu.VMEM((HEADS // 2, SLOTS, LANES), BF)
    return pl.pallas_call(
        main_kernel,
        out_shape=jax.ShapeDtypeStruct((SLOTS, D), BF),
        in_specs=[pl.BlockSpec(memory_space=pltpu.SMEM)] + [VMEM] * (6 + len(parts)),
        out_specs=VMEM,
        scratch_shapes=[
            wide,
            pltpu.VMEM((D, 3 * D), BF),
            pltpu.VMEM((2 * D, D), BF),
            pairs,
            pairs,
            pltpu.VMEM((HEADS, LANES, SLOTS), BF),
            pltpu.VMEM((HEADS, D // HEADS + 16, SLOTS), BF),
            pairs,
        ],
        compiler_params=pltpu.CompilerParams(vmem_limit_bytes=48 * 2**20),
        name="rerank_lists",
        cost_estimate=pl.CostEstimate(flops=2**34, bytes_accessed=2**23, transcendentals=2**23),
    )(place, pay, users, cross, up, down, *parts, out_w)


def exchange(values):
    return lax.all_to_all(values, "cand", split_axis=0, concat_axis=0, tiled=True)


def along_y(steps):
    return [(i, (i + 2 * steps) % 16) for i in range(16)]


CORE = [(i, i ^ 1) for i in range(16)]


def gather_projection(part, opposite):
    pair = jnp.concatenate([part, opposite], axis=0)
    two = lax.ppermute(pair, "req", along_y(6))
    one = lax.ppermute(pair, "req", along_y(7))
    seven = lax.ppermute(pair, "req", along_y(1))
    near = (pair, one, seven, two)
    return near + tuple(lax.ppermute(piece, "req", CORE) for piece in near)


def local(
    cand_rows,
    user_rows,
    row_owner,
    row_list,
    cross_weight,
    up_weight,
    down_weight,
    project_in,
    project_out,
):
    opposite = lax.ppermute(project_in, "req", along_y(4))
    pay, pos = pack(cand_rows[0], row_owner.reshape(1, -1), row_list)
    arrived = exchange(pay)
    pick, opposite = lax.optimization_barrier((pick_matrix(pos), opposite))
    parts = gather_projection(project_in, opposite)
    req = lax.axis_index("req")
    place = jnp.stack([req // 2, req % 2]).astype(jnp.int32)
    result = rerank(
        place, arrived, user_rows[0], cross_weight, up_weight, down_weight, parts, project_out
    )
    back = exchange(result.reshape(PEERS, CAP, D))
    return dot(pick, back.reshape(SLOTS, D)).astype(BF)[None]


def solution(mesh):
    in_specs = (
        P("req", "cand", None),
        P("req", "cand", None),
        P("req", "cand", None),
        P("req", "cand"),
        P(),
        P(),
        P(),
        P("req", None),
        P(),
    )
    out_specs = P("req", "cand", None)
    return jax.shard_map(local, mesh=mesh, in_specs=in_specs, out_specs=out_specs, check_vma=False)
```

```python
import jax
import jax.numpy as jnp
from jax import lax
from jax.experimental import pallas as pl
from jax.experimental.pallas import tpu as pltpu
from jax.sharding import PartitionSpec as P

HEADS = 8
PEERS = 32
CAP = 32
SLOTS = PEERS * CAP
D = 512
LANES = 128
COLS = D // LANES
PAY = COLS * CAP + 8
QBLOCK = 512
APART = 1024.0
BF = jnp.bfloat16
F32 = jnp.float32
VMEM = pl.BlockSpec(memory_space=pltpu.VMEM)
ANY = pl.BlockSpec(memory_space=pl.ANY)
PARTS = 4
STEPS = (0, 4, 1, 5, 7, 3, 2, 6)
NT = (((1,), (1,)), ((), ()))


def iota(shape, dim):
    return lax.broadcasted_iota(jnp.int32, shape, dim)


def ones_where(cond):
    return jnp.where(cond, 1.0, 0.0).astype(BF)


def dot(a, b):
    return jnp.dot(a, b, preferred_element_type=F32)


def pack_kernel(rows_hbm, owner_hbm, list_hbm, pay_hbm, pos_hbm, rows_ref, owner_ref, list_ref, pay_ref, pos_ref, sems, sent_sems):
    fetch = [
        pltpu.make_async_copy(owner_hbm, owner_ref, sems.at[0]),
        pltpu.make_async_copy(list_hbm, list_ref, sems.at[1]),
        pltpu.make_async_copy(rows_hbm, rows_ref, sems.at[2]),
    ]
    for copy in fetch:
        copy.start()
    rows = rows_ref.shape[0]
    upto = ones_where(iota((rows, rows), 0) <= iota((rows, rows), 1))
    fetch[0].wait()
    owner = owner_ref[...]
    mine = iota((PEERS, rows), 0) == owner
    count = dot(ones_where(mine), upto)
    rank = jnp.sum(jnp.where(mine, count, 0.0), axis=0, keepdims=True).astype(jnp.int32) - 1
    pos = owner * CAP + rank
    pos_ref[...] = pos
    leave = [pltpu.make_async_copy(pos_ref, pos_hbm, sems.at[3])]
    leave[0].start()
    fetch[1].wait()
    tags = jnp.where(mine, (list_ref[...] + 1).astype(F32), 0.0).astype(BF)
    at_rank = ones_where(iota((LANES, rows), 0) == rank)
    tag_rows = lax.dot_general(tags, at_rank, NT, preferred_element_type=F32)
    pay_ref[:, COLS * CAP :, :] = jnp.broadcast_to(
        tag_rows[:, None, :], (PEERS, PAY - COLS * CAP, LANES)
    ).astype(BF)
    fetch[2].wait()
    for part in range(PARTS):
        width = SLOTS // PARTS
        place = ones_where(iota((width, rows), 0) + part * width == pos)
        sent = dot(place, rows_ref[...]).astype(BF)
        peers = pl.ds(part * (PEERS // PARTS), PEERS // PARTS)
        for c in range(COLS):
            pay_ref[peers, c * CAP : (c + 1) * CAP, :] = sent[:, c * LANES : (c + 1) * LANES].reshape(
                PEERS // PARTS, CAP, LANES
            )
        copy = pltpu.make_async_copy(pay_ref.at[peers], pay_hbm.at[peers], sent_sems.at[part])
        copy.start()
        leave.append(copy)
    for copy in leave:
        copy.wait()


def pack(rows, owner, lists):
    return pl.pallas_call(
        pack_kernel,
        out_shape=(
            jax.ShapeDtypeStruct((PEERS, PAY, LANES), BF),
            jax.ShapeDtypeStruct(owner.shape, jnp.int32),
        ),
        in_specs=[ANY] * 3,
        out_specs=(ANY, ANY),
        scratch_shapes=[
            pltpu.VMEM(rows.shape, BF),
            pltpu.VMEM(owner.shape, jnp.int32),
            pltpu.VMEM(lists.shape, jnp.int32),
            pltpu.VMEM((PEERS, PAY, LANES), BF),
            pltpu.VMEM(owner.shape, jnp.int32),
            pltpu.SemaphoreType.DMA((4,)),
            pltpu.SemaphoreType.DMA((PARTS,)),
        ],
        name="pack_rows",
        cost_estimate=pl.CostEstimate(flops=2**29, bytes_accessed=2**21, transcendentals=0),
    )(rows, owner, lists)


def pick_kernel(pos_ref, pick_ref):
    rows = pick_ref.shape[0]
    pos = pos_ref[...].astype(F32)
    column = jnp.sum(
        jnp.where(iota((rows, rows), 0) == iota((rows, rows), 1), pos, 0.0), axis=1, keepdims=True
    ).astype(jnp.int32)
    pick_ref[...] = ones_where(iota(pick_ref.shape, 1) == column)


def pick_matrix(pos):
    return pl.pallas_call(
        pick_kernel,
        out_shape=jax.ShapeDtypeStruct((pos.shape[1], SLOTS), BF),
        in_specs=[VMEM],
        out_specs=VMEM,
        name="pick_matrix",
        cost_estimate=pl.CostEstimate(flops=2**36, bytes_accessed=2**28, transcendentals=0),
    )(pos)


def main_kernel(
    y_ref,
    pay_ref,
    user_ref,
    cross_ref,
    up_ref,
    down_ref,
    *refs,
):
    part_refs, (out_w_ref, out_ref) = refs[:8], refs[8:10]
    mixed_ref, in_ref, in_t, even_k, odd_k, queries_ref, values_ref, attended_ref = refs[10:]
    share = part_refs[0].shape[0] // 2
    y, core = y_ref[0], y_ref[1]
    for i, step in enumerate(STEPS):
        chip = lax.rem(y + step, 8) * 2
        for ref, which in ((part_refs[i // 2], core), (part_refs[4 + i // 2], 1 - core)):
            spot = pl.multiple_of((chip + which) * share, share)
            in_ref[pl.ds(spot, share), :] = ref[i % 2 * share : (i % 2 + 1) * share, :]

    head = D // HEADS
    lane = iota((SLOTS, LANES), 1)
    low = lane < head
    fit = lane == lax.rem(iota((SLOTS, LANES), 0), CAP)
    spread = ones_where(iota((LANES, LANES), 0) >= 0)
    mean = jnp.where(
        iota((256, 256), 0) // head == iota((256, 256), 1) // head, 1.0 / head, 0.0
    ).astype(BF)

    tag8 = pay_ref[:, COLS * CAP :, :].astype(F32)
    tag32 = jnp.concatenate([tag8] * (CAP // 8), axis=1).reshape(SLOTS, LANES)
    tag_bf = jnp.where(fit, tag32, 0.0).astype(BF)
    tag = dot(tag_bf, spread)
    tag_t = lax.dot_general(spread[:head], tag_bf, NT, preferred_element_type=F32)
    first, second = tag == 1.0, tag == 2.0
    combined = []
    for c in range(COLS):
        cut = slice(c * LANES, (c + 1) * LANES)
        x = pay_ref[:, c * CAP : (c + 1) * CAP, :].reshape(SLOTS, LANES).astype(F32)
        user = jnp.where(second, user_ref[1:2, cut].astype(F32), user_ref[0:1, cut].astype(F32))
        combined.append((x + user).astype(BF))
    combined = jnp.concatenate(combined, axis=1)
    wide = combined.astype(F32)
    crossed = (wide * dot(combined, cross_ref[...]) + wide).astype(BF)
    active = jnp.maximum(dot(crossed, up_ref[...]), 0.0).astype(BF)
    mixed = (crossed.astype(F32) + dot(active, down_ref[...])).astype(BF)
    mixed_ref[...] = mixed

    in_t[...] = jnp.concatenate([in_ref[:, :D].T, in_ref[:, 2 * D :].T], axis=0)
    keys = dot(mixed, in_ref[:, D : 2 * D])
    square = (keys * keys).astype(BF)
    spot = lax.rem(lane, head)
    key_mark = jnp.where(
        jnp.logical_or(
            jnp.logical_and(spot == 0, jnp.logical_not(first)),
            jnp.logical_and(spot == 1, jnp.logical_not(second)),
        ),
        1.0,
        0.0,
    )
    for j in range(D // 256):
        cut = slice(j * 256, (j + 1) * 256)
        normed = keys[:, cut] * lax.rsqrt(dot(square[:, cut], mean) + 1e-06)
        for i in range(2):
            key = normed[:, i * LANES : (i + 1) * LANES]
            even_k[2 * j + i, :, :] = jnp.where(low, key, key_mark).astype(BF)
            odd_k[2 * j + i, :, :] = jnp.where(low, key_mark, key).astype(BF)

    turned = lax.dot_general(in_t[...], mixed, NT, preferred_element_type=F32)
    row = iota((head, SLOTS), 0)
    query_mark = jnp.where(
        jnp.logical_or(
            jnp.logical_and(row == 0, tag_t == 1.0), jnp.logical_and(row == 1, tag_t == 2.0)
        ),
        -APART,
        0.0,
    ).astype(BF)
    for h in range(HEADS):
        query = turned[h * head : (h + 1) * head, :]
        level = jnp.mean(query * query, axis=0, keepdims=True)
        query = (query * (lax.rsqrt(level + 1e-06) * head**-0.5)).astype(BF)
        at = h % 2 * head
        queries_ref[h, at : at + head, :] = query
        queries_ref[h, head - at : 2 * head - at, :] = query_mark
        values_ref[h, :head, :] = turned[D + h * head : D + (h + 1) * head, :].astype(BF)
        values_ref[h, head:, :] = ones_where(iota((16, SLOTS), 0) >= 0)

    for p in range(HEADS // 2):
        pair = []
        for i, k in enumerate((even_k, odd_k)):
            h = 2 * p + i
            halves = []
            for j in range(SLOTS // QBLOCK):
                cut = slice(j * QBLOCK, (j + 1) * QBLOCK)
                powered = jnp.exp(dot(k[p], queries_ref[h, :, cut])).astype(BF)
                summed = dot(values_ref[h], powered)
                halves.append((summed[:head] * (1.0 / summed[head : head + 1])).astype(BF))
            pair.append(jnp.concatenate(halves, axis=1))
        attended_ref[p] = jnp.concatenate(pair, axis=0).T

    attended = jnp.concatenate([attended_ref[p] for p in range(HEADS // 2)], axis=1)
    out_ref[...] = (mixed_ref[...].astype(F32) + dot(attended, out_w_ref[...])).astype(BF)


def rerank(place, pay, users, cross, up, down, parts, out_w):
    wide = pltpu.VMEM((SLOTS, D), BF)
    pairs = pltpu.VMEM((HEADS // 2, SLOTS, LANES), BF)
    return pl.pallas_call(
        main_kernel,
        out_shape=jax.ShapeDtypeStruct((SLOTS, D), BF),
        in_specs=[pl.BlockSpec(memory_space=pltpu.SMEM)] + [VMEM] * (6 + len(parts)),
        out_specs=VMEM,
        scratch_shapes=[
            wide,
            pltpu.VMEM((D, 3 * D), BF),
            pltpu.VMEM((2 * D, D), BF),
            pairs,
            pairs,
            pltpu.VMEM((HEADS, LANES, SLOTS), BF),
            pltpu.VMEM((HEADS, D // HEADS + 16, SLOTS), BF),
            pairs,
        ],
        compiler_params=pltpu.CompilerParams(vmem_limit_bytes=48 * 2**20),
        name="rerank_lists",
        cost_estimate=pl.CostEstimate(flops=2**34, bytes_accessed=2**23, transcendentals=2**23),
    )(place, pay, users, cross, up, down, *parts, out_w)


def exchange(values):
    return lax.all_to_all(values, "cand", split_axis=0, concat_axis=0, tiled=True)


def along_y(steps):
    return [(i, (i + 2 * steps) % 16) for i in range(16)]


CORE = [(i, i ^ 1) for i in range(16)]


def gather_projection(part, opposite):
    pair = jnp.concatenate([part, opposite], axis=0)
    two = lax.ppermute(pair, "req", along_y(6))
    one = lax.ppermute(pair, "req", along_y(7))
    seven = lax.ppermute(pair, "req", along_y(1))
    near = (pair, one, seven, two)
    return near + tuple(lax.ppermute(piece, "req", CORE) for piece in near)


def local(
    cand_rows,
    user_rows,
    row_owner,
    row_list,
    cross_weight,
    up_weight,
    down_weight,
    project_in,
    project_out,
):
    opposite = lax.ppermute(project_in, "req", along_y(4))
    pay, pos = pack(cand_rows[0], row_owner.reshape(1, -1), row_list)
    arrived = exchange(pay)
    pick, opposite = lax.optimization_barrier((pick_matrix(pos), opposite))
    parts = gather_projection(project_in, opposite)
    req = lax.axis_index("req")
    place = jnp.stack([req // 2, req % 2]).astype(jnp.int32)
    result = rerank(
        place, arrived, user_rows[0], cross_weight, up_weight, down_weight, parts, project_out
    )
    back = exchange(result.reshape(PEERS, CAP, D))
    return dot(pick, back.reshape(SLOTS, D)).astype(BF)[None]


def solution(mesh):
    in_specs = (
        P("req", "cand", None),
        P("req", "cand", None),
        P("req", "cand", None),
        P("req", "cand"),
        P(),
        P(),
        P(),
        P("req", None),
        P(),
    )
    out_specs = P("req", "cand", None)
    return jax.shard_map(local, mesh=mesh, in_specs=in_specs, out_specs=out_specs, check_vma=False)
```
